32 devices in a mesh: blk: 8 (over y, x, core), rep: 4 (over z).
Axes of the slice: x: 2, y: 2, z: 4, core: 2. Of those that a mesh axis runs over, the one named last changes fastest.
Arguments:
- queries: bfloat16 [8192, 4096], P(('blk', 'rep')), as said below
- query_group: int32 [8192, 1], P(('blk', 'rep')), may hold values from 0 to 3; in each aligned block of 256 rows (0 to 255, 256 to 511, ...) at most 128 rows name the same one
- query_bin: int32 [8192], P(('blk', 'rep')), may hold values from 0 to 63
- query_shift: int32 [8192], P(('blk', 'rep')), may hold values from 1 to 2
- library: bfloat16 [4, 256, 4096], P('rep', 'blk'), as said below
- library_bin: int32 [4, 256], P('rep', 'blk'), may hold values from 0 to 63
Outputs:
- best_scores: float32 [8192, 8], P(('blk', 'rep'))
The draws below stay inside these ranges and needn't reach their ends.
Inputs may be any that keep to these rules, and one draw needn't show every extreme that they name: `query_group`: among the 256 queries of one device at most 128 name the same group, and on every draw some device has a group named by exactly 128 of its queries. `queries`: intensities are nonnegative and every spectrum has peaks. `library`: intensities are nonnegative and every spectrum has peaks.
All inputs are finite; a program needn't handle non-finite values.
Results may differ from the reference program's by a relative error of at most 0.0021.
Values may be sent and summed in bfloat16 or wider, within the bound.
A program may use at most 192 MiB of HBM per device.

```python
import math
import jax
import jax.numpy as jnp
import numpy as np
from jax import lax

W = 4096
Q_DEV = 256
K = 8
NSHIFT = 2
SHIFT_BINS = 16
GBINS = 64
WIN = 16
GROUPS = 4
CAP = 128
QUERIES = 8192
LIB_G = 256


def spectra(key, shape):
    k_one, k_two, k_three = jax.random.split(key, 3)
    present = jax.random.uniform(k_one, shape) < 0.3
    peak = jnp.exp(2.5 * jax.random.normal(k_two, shape, jnp.float32))
    scale = jnp.exp(jax.random.uniform(k_three, shape[:-1] + (1,), jnp.float32, 0.0, math.log(10.0)))
    first = jnp.zeros(shape, jnp.float32).at[..., 7].set(1.0)
    values = jnp.where(present, peak * scale, 0.0) + first * scale
    return values.astype(jnp.float32)


def draw_queries(key, part):
    return spectra(jax.random.fold_in(key, 11), (QUERIES, W)).astype(jnp.bfloat16)


def draw_library(key, part):
    return spectra(jax.random.fold_in(key, 23), (GROUPS, LIB_G, W)).astype(jnp.bfloat16)


def set_ends(array, key, low, high):
    longest = array.shape.index(max(array.shape))
    spots = []
    for shift in (0, 1):
        where = [jax.random.randint(jax.random.fold_in(key, axis), (), 0, length) for axis, length in enumerate(array.shape)]
        where[longest] = (where[longest] + shift) % array.shape[longest]
        spots.append(tuple(where))
    return array.at[spots[0]].set(low).at[spots[1]].set(high)


def routed_block(own_key, own, number, rows, count, top, bound, lean):
    ranking = jax.random.permutation(own_key, count)
    packed, common = shares(count, rows * top, bound, lean, True), shares(count, rows * top, bound, lean, False)
    places = jnp.arange(count)

    def named(tallies, turn):
        used = int((tallies > 0).sum())
        fixed = max(1, used // 4)
        moved = fixed + (places - fixed + turn * (used - fixed)) % max(1, count - fixed)
        return jnp.zeros((count,), jnp.int32).at[ranking[jnp.where(places < fixed, places, moved)]].set(jnp.asarray(tallies, jnp.int32))

    tallies = jnp.where(number % 4 == 0, named(packed, number // 4), named(common, number - number // 4 - 1))
    mixed = jax.random.permutation(jax.random.fold_in(own, 3), count)
    source_of, sink = mixed[0:count // 2 * 2:2], mixed[1:count // 2 * 2:2]
    room = jnp.minimum(tallies[source_of] - 1, bound - tallies[sink]) // 2
    room = jnp.where((source_of == ranking[0]) | (sink == ranking[0]) | (tallies[sink] == 0), 0, jnp.maximum(room, 0))
    moved = jax.random.randint(jax.random.fold_in(own, 4), (count // 2,), 0, 1 << 20) % (room + 1)
    tallies = tallies.at[source_of].add(-moved).at[sink].add(moved)
    items = jnp.searchsorted(jnp.cumsum(tallies), jnp.arange(rows * top), side="right").astype(jnp.int32)
    listing = items.reshape(top, rows).T
    listing = listing[jax.random.permutation(jax.random.fold_in(own, 1), rows)]
    turn = jax.random.randint(jax.random.fold_in(own, 2), (rows, 1), 0, top)
    return jnp.take_along_axis(listing, (jnp.arange(top)[None, :] + turn) % top, axis=1)


def shares(number_of, total, reach, lean, full):
    portions = [(1 << 20) // math.isqrt(standing ** lean) + 1 for standing in range(1, number_of + 1)]
    largest = reach if full else min(reach, max(-(-total // number_of), total * portions[0] // sum(portions)))
    least = 1 if total - largest >= number_of - 1 else 0
    holding, spare = [largest] + [least] * (number_of - 1), total - largest - least * (number_of - 1)
    while spare > 0:
        free = [i for i in range(1, number_of) if holding[i] < largest] or [i for i in range(1, number_of) if holding[i] < reach]
        pool, left = sum([portions[i] for i in free]), spare
        for i in free:
            extra = min(reach - holding[i], max(1, left * portions[i] // pool), spare)
            holding[i] = holding[i] + extra
            spare = spare - extra
    return np.array(holding)


def setup_inputs(seed: int = 0) -> dict:
    keys = jax.random.split(jax.random.key(seed), 7)
    queries = draw_queries(jax.random.fold_in(keys[6], 71), 0)
    query_group_keys = jax.random.split(jax.random.fold_in(keys[1], 1), QUERIES // Q_DEV)
    query_group_turns = jax.random.permutation(jax.random.fold_in(keys[1], 3), QUERIES // Q_DEV)
    query_group = jax.vmap(lambda own, number: routed_block(jax.random.fold_in(keys[1], 2), own, number, Q_DEV, GROUPS, 1, CAP, 2))(query_group_keys, query_group_turns).reshape((QUERIES, 1))
    query_bin = set_ends(jax.random.randint(keys[2], (QUERIES,), 0, GBINS), jax.random.fold_in(keys[2], 1), 0, GBINS - 1).astype(jnp.int32)
    query_shift = set_ends(jax.random.randint(keys[3], (QUERIES,), 1, NSHIFT + 1), jax.random.fold_in(keys[3], 1), 1, NSHIFT).astype(jnp.int32)
    library = draw_library(jax.random.fold_in(keys[6], 71), 0)
    library_bin = set_ends(jax.random.randint(keys[5], (GROUPS, LIB_G), 0, GBINS), jax.random.fold_in(keys[5], 1), 0, GBINS - 1).astype(jnp.int32)
    return {"queries": queries, "query_group": query_group, "query_bin": query_bin, "query_shift": query_shift, "library": library, "library_bin": library_bin}


def unit_rows(raw):
    values = jnp.sqrt(raw.astype(jnp.float32))
    total = lax.optimization_barrier(jnp.sum(values * values, axis=-1, keepdims=True))
    return (values * lax.rsqrt(total + 1e-06)).astype(jnp.bfloat16)

def lower_bins(rows, amount):
    tail = jnp.zeros(rows.shape[:-1] + (amount,), rows.dtype)
    return jnp.concatenate([rows[..., amount:], tail], axis=-1)

def slot_index(group, groups, capacity):
    labels = jnp.arange(groups, dtype=jnp.int32)
    onehot = (group[:, None] == labels[None, :]).astype(jnp.int32)
    before = jnp.cumsum(onehot, axis=0) - onehot
    place = lax.optimization_barrier(jnp.sum(before * onehot, axis=1)).astype(jnp.int32)
    return (group * capacity + place).astype(jnp.int32)

def slot_source(slot, count, slots):
    start = jnp.full((slots,), count, jnp.int32)
    return start.at[slot].set(jnp.arange(count, dtype=jnp.int32))

def reference(queries, query_group, query_bin, query_shift, library, library_bin):
    blocks = QUERIES // Q_DEV
    slots = GROUPS * CAP
    unit_q = unit_rows(queries).reshape(blocks, Q_DEV, W)
    group = query_group[:, 0].reshape(blocks, Q_DEV)
    bins = query_bin.reshape(blocks, Q_DEV)
    shifts = query_shift.reshape(blocks, Q_DEV)
    slot = jax.vmap(lambda g: slot_index(g, GROUPS, CAP))(group)
    source = jax.vmap(lambda s: slot_source(s, Q_DEV, slots))(slot)
    pad_q = jnp.concatenate([unit_q, jnp.zeros((blocks, 1, W), unit_q.dtype)], axis=1)
    pad_bin = jnp.concatenate([bins, jnp.zeros((blocks, 1), jnp.int32)], axis=1)
    pad_shift = jnp.concatenate([shifts, jnp.zeros((blocks, 1), jnp.int32)], axis=1)
    take = jax.vmap(lambda a, i: a[i])
    slot_q = take(pad_q, source).reshape(blocks, GROUPS, CAP, W)
    slot_bin = take(pad_bin, source).reshape(blocks, GROUPS, CAP)
    slot_shift = take(pad_shift, source).reshape(blocks, GROUPS, CAP)
    unit_lib = unit_rows(library)
    results = []
    for g in range(GROUPS):
        lib_f = unit_lib[g].astype(jnp.float32)
        lib_bin = library_bin[g]

        def per_block(item):
            rows, qbin, qshift = item
            moved = jnp.zeros_like(rows)
            for s in range(1, NSHIFT + 1):
                moved = jnp.where((qshift == s)[:, None], lower_bins(rows, s * SHIFT_BINS), moved)
            both = jnp.concatenate([rows, moved], axis=0).astype(jnp.float32)
            prod = jnp.dot(lib_f, both.T, preferred_element_type=jnp.float32)
            plain = prod[:, :CAP]
            shifted = prod[:, CAP:]
            near = jnp.abs(lib_bin[:, None] - qbin[None, :]) <= WIN
            score = jnp.where(near, jnp.maximum(plain, shifted), 0.0)
            return lax.top_k(score.T, K)[0]
        results.append(lax.map(per_block, (slot_q[:, g], slot_bin[:, g], slot_shift[:, g])))
    stacked = jnp.stack(results, axis=1).reshape(blocks, slots, K)
    best = take(stacked, slot)
    return best.reshape(QUERIES, K)
```

```python
import functools

import jax
import jax.numpy as jnp
from jax import lax
from jax.experimental import pallas as pl
from jax.experimental.pallas import tpu as pltpu
from jax.sharding import PartitionSpec as P

W = 4096
K = 8
NSHIFT = 2
SHIFT_BINS = 16
WIN = 16
LANES = 128
MESH = pl.DeviceIdType.MESH


def unit_rows(raw):
    values = jnp.sqrt(raw.astype(jnp.float32))
    total = jnp.sum(values * values, axis=-1, keepdims=True)
    return (values * lax.rsqrt(total + 1e-06)).astype(jnp.bfloat16)


def lower_bins(rows, amount):
    tail = jnp.zeros(rows.shape[:-1] + (amount,), rows.dtype)
    return jnp.concatenate([rows[..., amount:], tail], axis=-1)


def general(queries, query_group, query_bin, query_shift, library, library_bin):
    unit_q = unit_rows(queries)
    moved = jnp.zeros_like(unit_q)
    for s in range(1, NSHIFT + 1):
        moved = jnp.where((query_shift == s)[:, None], lower_bins(unit_q, s * SHIFT_BINS), moved)
    both = jnp.concatenate([unit_q, moved], axis=0)
    lib = lax.all_gather(unit_rows(library), "blk", axis=1, tiled=True)
    lib = lax.all_gather(lib, "rep", axis=0, tiled=True)
    bins = lax.all_gather(library_bin, "blk", axis=1, tiled=True)
    bins = lax.all_gather(bins, "rep", axis=0, tiled=True)
    n_q = queries.shape[0]
    score = jnp.zeros((n_q, lib.shape[1]), jnp.float32)
    for g in range(lib.shape[0]):
        prod = lax.dot_general(
            both, lib[g], (((1,), (1,)), ((), ())), preferred_element_type=jnp.float32
        )
        near = jnp.abs(query_bin[:, None] - bins[g][None, :]) <= WIN
        high = jnp.where(near, jnp.maximum(prod[:n_q], prod[n_q:]), 0.0)
        score = jnp.where(query_group == g, high, score)
    position = lax.broadcasted_iota(jnp.int32, score.shape, 1)
    picked = []
    for _ in range(K):
        top = jnp.max(score, axis=1, keepdims=True)
        first = jnp.min(jnp.where(score == top, position, score.shape[1]), axis=1, keepdims=True)
        picked.append(top)
        score = jnp.where(position == first, -3e38, score)
    return jnp.concatenate(picked, axis=1)


def fast_kernel(
    n_rep, rows, q_hbm, lib_ref, libbin_ref, grp_ref, bin_ref, shift_ref, out_ref,
    lib, qraw, qval, qt, best, q_sem,
    zs, zr, xs, xr, ys, yr, xds, xdr, yds, ydr, ss, sr,
):
    b = lax.axis_index("blk")
    z = lax.axis_index("rep")
    core = b % 2
    bx = (b // 2) % 2
    by = b // 4
    sib = b + 1 - 2 * core
    xn = b + 2 - 4 * bx
    yn = b + 4 - 8 * by
    dn = xn + 4 - 8 * by
    half = rows // 2

    qcopy = pltpu.make_async_copy(q_hbm, qraw, q_sem)
    qcopy.start()

    barrier = pltpu.get_barrier_semaphore()
    for other in (sib, xn, yn):
        pl.semaphore_signal(barrier, inc=1, device_id=(other, z), device_id_type=MESH)

    @pl.when(z > 0)
    def _():
        pl.semaphore_signal(barrier, inc=1, device_id=(b, z - 1), device_id_type=MESH)

    @pl.when(z < n_rep - 1)
    def _():
        pl.semaphore_signal(barrier, inc=1, device_id=(b, z + 1), device_id_type=MESH)

    vals = jnp.sqrt(lib_ref[0].astype(jnp.float32))
    total = jnp.sum(vals * vals, axis=-1, keepdims=True)
    mine = pl.ds(pl.multiple_of(b * rows, rows), rows)
    lib[z, mine, 0:W] = (vals * lax.rsqrt(total + 1e-06)).astype(jnp.bfloat16)
    r_id = lax.broadcasted_iota(jnp.int32, (rows, rows), 0)
    c_id = lax.broadcasted_iota(jnp.int32, (rows, rows), 1)
    spread = jnp.where(r_id == c_id, libbin_ref[...].astype(jnp.float32), 0.0)
    column = jnp.sum(spread, axis=1, keepdims=True)
    lib[z, mine, W : W + LANES] = jnp.broadcast_to(column, (rows, LANES)).astype(jnp.bfloat16)

    ends = jnp.where(z == 0, 1, 0) + jnp.where(z == n_rep - 1, 1, 0)
    pl.semaphore_wait(barrier, 5 - ends)

    def order(j):
        m = z // (n_rep // 2)
        zz = z + m * (n_rep - 1 - 2 * z)
        o = jnp.where(j == 0, zz, jnp.where(j == 1, 1 - zz, j))
        return o + m * (n_rep - 1 - 2 * o)

    def shard(p, blk):
        return lib.at[p, pl.ds(pl.multiple_of(blk * rows, rows), rows)]

    def part(p, blk, h):
        return lib.at[p, pl.ds(pl.multiple_of(blk * rows + h * half, half), half)]

    def copy(ref, send, recv, dev):
        return pltpu.make_async_remote_copy(
            src_ref=ref, dst_ref=ref, send_sem=send, recv_sem=recv,
            device_id=dev, device_id_type=MESH,
        )

    def z_up(p):
        return copy(shard(p, b), zs.at[0, p], zr.at[p], (b, z + 1))

    def z_down(p):
        return copy(shard(p, b), zs.at[1, p], zr.at[p], (b, z - 1))

    def x_own(p, blk):
        return copy(shard(p, blk), xs.at[p], xr.at[p], (xn, z))

    def y_own(p, blk):
        return copy(shard(p, blk), ys.at[p], yr.at[p], (yn, z))

    def x_diag(p, blk):
        return copy(part(p, blk, 1), xds.at[p], xdr.at[p], (xn, z))

    def y_diag(p, blk):
        return copy(part(p, blk, 0), yds.at[p], ydr.at[p], (yn, z))

    def to_sib(p, blk, slot):
        return copy(shard(p, blk), ss.at[p, slot], sr.at[p, slot], (sib, z))

    def away(p, do):
        @pl.when((p <= z) & (z < n_rep - 1))
        def _():
            do(z_up(p))

        @pl.when((p >= z) & (z > 0))
        def _():
            do(z_down(p))

    def begin(c):
        c.start()

    def spread_own(p):
        away(p, begin)
        x_own(p, b).start()
        y_own(p, b).start()
        to_sib(p, b, 0).start()

    spread_own(z)

    qcopy.wait()
    step = 512

    def load(i, acc):
        cols = pl.ds(pl.multiple_of(i * step, step), step)
        v = jnp.sqrt(qraw[:, cols].astype(jnp.float32).T)
        qval[cols, :] = v
        return acc + jnp.sum(v * v, axis=0, keepdims=True)

    n_q = qraw.shape[0]
    q_total = lax.fori_loop(0, W // step, load, jnp.zeros((1, n_q), jnp.float32))
    scale = lax.rsqrt(q_total + 1e-06)

    def norm(i, c):
        at = pl.ds(pl.multiple_of(i * step, step), step)
        qt[at, 0:n_q] = (qval[at, :] * scale).astype(jnp.bfloat16)
        return c

    lax.fori_loop(0, W // step, norm, 0)
    qt[pl.ds(W, 2 * SHIFT_BINS), 0:n_q] = jnp.zeros((2 * SHIFT_BINS, n_q), jnp.bfloat16)
    one = shift_ref[...] == 1

    def move(i, c):
        base = pl.multiple_of(i * step, step)
        near = qt[pl.ds(base + SHIFT_BINS, step), 0:n_q].astype(jnp.float32)
        far = qt[pl.ds(base + 2 * SHIFT_BINS, step), 0:n_q].astype(jnp.float32)
        qt[pl.ds(base, step), n_q : 2 * n_q] = jnp.where(one, near, far).astype(jnp.bfloat16)
        return c

    lax.fori_loop(0, W // step, move, 0)
    best[...] = jnp.zeros_like(best)

    def compute(p):
        for slot, blk in enumerate((b, xn, yn, dn)):
            to_sib(p, blk, slot).wait_recv()
        prod = jnp.dot(lib[p, :, 0:W], qt[0:W, :], preferred_element_type=jnp.float32)
        high = jnp.maximum(prod[:, 0:n_q], prod[:, n_q : 2 * n_q])
        bins = lib[p, :, W : W + LANES].astype(jnp.float32)
        bins = jnp.concatenate([bins] * (n_q // LANES), axis=1)
        near = jnp.abs(bins - bin_ref[...].astype(jnp.float32)) <= float(WIN)
        score = jnp.where(near, high, 0.0)
        best[...] = jnp.where(grp_ref[...] == p, score, best[...])

    def stage(t, c):
        @pl.when(t < n_rep)
        def _():
            p = order(t)
            z_up(p).wait_recv()
            spread_own(p)

        @pl.when(t <= n_rep)
        def _():
            p = order(t - 1)
            x_own(p, b).wait_recv()
            y_diag(p, xn).start()
            to_sib(p, xn, 1).start()
            y_own(p, b).wait_recv()
            x_diag(p, yn).start()
            to_sib(p, yn, 2).start()

        @pl.when((t >= 2) & (t <= n_rep + 1))
        def _():
            p = order(t - 2)
            x_diag(p, dn).wait_recv()
            y_diag(p, dn).wait_recv()
            to_sib(p, dn, 3).start()

        @pl.when(t >= 3)
        def _():
            compute(order(t - 3))

        return c

    lax.fori_loop(1, n_rep + 3, stage, 0)

    position = lax.broadcasted_iota(jnp.int32, (K, n_q), 0)
    result = jnp.zeros((K, n_q), jnp.float32)
    filled = jnp.zeros((1, n_q), jnp.int32)
    for _ in range(K):
        cur = best[...]
        top = jnp.max(cur, axis=0, keepdims=True)
        same = cur == top
        count = jnp.sum(same.astype(jnp.int32), axis=0, keepdims=True)
        best[...] = jnp.where(same, -3e38, cur)
        result = jnp.where(position >= filled, top, result)
        filled = filled + count
    out_ref[...] = result

    def finish(p, c):
        away(p, lambda d: d.wait_send())
        x_own(p, b).wait_send()
        y_own(p, b).wait_send()
        y_diag(p, xn).wait_send()
        x_diag(p, yn).wait_send()
        for slot, blk in enumerate((b, xn, yn, dn)):
            to_sib(p, blk, slot).wait_send()
        return c

    lax.fori_loop(0, n_rep, finish, 0)


def fast(n_rep, queries, query_group, query_bin, query_shift, library, library_bin):
    n_q = queries.shape[0]
    rows = library.shape[1]
    lib_g = 8 * rows
    dma = pltpu.SemaphoreType.DMA
    vmem = pl.BlockSpec(memory_space=pltpu.VMEM)
    top = pl.pallas_call(
        functools.partial(fast_kernel, n_rep, rows),
        out_shape=jax.ShapeDtypeStruct((K, n_q), jnp.float32),
        in_specs=[pl.BlockSpec(memory_space=pl.ANY)] + [vmem] * 5,
        out_specs=vmem,
        scratch_shapes=[
            pltpu.VMEM((n_rep, lib_g, W + LANES), jnp.bfloat16),
            pltpu.VMEM((n_q, W), jnp.bfloat16),
            pltpu.VMEM((W, n_q), jnp.float32),
            pltpu.VMEM((W + 2 * SHIFT_BINS, 2 * n_q), jnp.bfloat16),
            pltpu.VMEM((lib_g, n_q), jnp.float32),
            dma(()),
            dma((2, n_rep)), dma((n_rep,)),
            dma((n_rep,)), dma((n_rep,)), dma((n_rep,)), dma((n_rep,)),
            dma((n_rep,)), dma((n_rep,)), dma((n_rep,)), dma((n_rep,)),
            dma((n_rep, 4)), dma((n_rep, 4)),
        ],
        compiler_params=pltpu.CompilerParams(
            collective_id=0, has_side_effects=True, vmem_limit_bytes=48 * 1024 * 1024
        ),
    )(
        queries,
        library,
        library_bin,
        query_group.reshape(1, n_q),
        query_bin.reshape(1, n_q),
        query_shift.reshape(1, n_q),
    )
    return top.T


def solution(mesh):
    in_specs = (
        P(("blk", "rep"), None),
        P(("blk", "rep"), None),
        P(("blk", "rep")),
        P(("blk", "rep")),
        P("rep", "blk", None),
        P("rep", "blk"),
    )
    out_specs = P(("blk", "rep"), None)
    if mesh.shape["blk"] == 8 and mesh.shape["rep"] == 4:
        body = functools.partial(fast, mesh.shape["rep"])
    else:
        body = general
    return jax.shard_map(
        body, mesh=mesh, in_specs=in_specs, out_specs=out_specs, check_vma=False
    )
```

```python
import functools

import jax
import jax.numpy as jnp
from jax import lax
from jax.experimental import pallas as pl
from jax.experimental.pallas import tpu as pltpu
from jax.sharding import PartitionSpec as P

W = 4096
K = 8
NSHIFT = 2
SHIFT_BINS = 16
WIN = 16
LANES = 128
MESH = pl.DeviceIdType.MESH


def unit_rows(raw):
    values = jnp.sqrt(raw.astype(jnp.float32))
    total = jnp.sum(values * values, axis=-1, keepdims=True)
    return (values * lax.rsqrt(total + 1e-06)).astype(jnp.bfloat16)


def lower_bins(rows, amount):
    tail = jnp.zeros(rows.shape[:-1] + (amount,), rows.dtype)
    return jnp.concatenate([rows[..., amount:], tail], axis=-1)


def general(queries, query_group, query_bin, query_shift, library, library_bin):
    unit_q = unit_rows(queries)
    moved = jnp.zeros_like(unit_q)
    for s in range(1, NSHIFT + 1):
        moved = jnp.where((query_shift == s)[:, None], lower_bins(unit_q, s * SHIFT_BINS), moved)
    both = jnp.concatenate([unit_q, moved], axis=0)
    lib = lax.all_gather(unit_rows(library), "blk", axis=1, tiled=True)
    lib = lax.all_gather(lib, "rep", axis=0, tiled=True)
    bins = lax.all_gather(library_bin, "blk", axis=1, tiled=True)
    bins = lax.all_gather(bins, "rep", axis=0, tiled=True)
    n_q = queries.shape[0]
    score = jnp.zeros((n_q, lib.shape[1]), jnp.float32)
    for g in range(lib.shape[0]):
        prod = lax.dot_general(
            both, lib[g], (((1,), (1,)), ((), ())), preferred_element_type=jnp.float32
        )
        near = jnp.abs(query_bin[:, None] - bins[g][None, :]) <= WIN
        high = jnp.where(near, jnp.maximum(prod[:n_q], prod[n_q:]), 0.0)
        score = jnp.where(query_group == g, high, score)
    position = lax.broadcasted_iota(jnp.int32, score.shape, 1)
    picked = []
    for _ in range(K):
        top = jnp.max(score, axis=1, keepdims=True)
        first = jnp.min(jnp.where(score == top, position, score.shape[1]), axis=1, keepdims=True)
        picked.append(top)
        score = jnp.where(position == first, -3e38, score)
    return jnp.concatenate(picked, axis=1)


def fast_kernel(
    n_rep, rows, q_hbm, lib_hbm, libbin_hbm, grp_hbm, bin_hbm, shift_hbm, out_ref,
    lib, qraw, qval, qt, best, lib_ref, libbin_ref, grp_ref, bin_ref, shift_ref, in_sem,
    zs, zr, xs, xr, ys, yr, xds, xdr, yds, ydr, ss, sr, zds, zdr, hs, hr,
):
    b = lax.axis_index("blk")
    z = lax.axis_index("rep")
    core = b % 2
    bx = (b // 2) % 2
    by = b // 4
    sib = b + 1 - 2 * core
    xn = b + 2 - 4 * bx
    yn = b + 4 - 8 * by
    dn = xn + 4 - 8 * by
    half = rows // 2

    pairs = (
        (lib_hbm, lib_ref), (libbin_hbm, libbin_ref), (q_hbm, qraw),
        (grp_hbm, grp_ref), (bin_hbm, bin_ref), (shift_hbm, shift_ref),
    )
    loads = [pltpu.make_async_copy(a, d, in_sem.at[i]) for i, (a, d) in enumerate(pairs)]
    for c in loads:
        c.start()

    barrier = pltpu.get_barrier_semaphore()
    for other in (sib, xn, yn):
        pl.semaphore_signal(barrier, inc=1, device_id=(other, z), device_id_type=MESH)

    @pl.when(z > 0)
    def _():
        pl.semaphore_signal(barrier, inc=1, device_id=(b, z - 1), device_id_type=MESH)

    @pl.when(z < n_rep - 1)
    def _():
        pl.semaphore_signal(barrier, inc=1, device_id=(b, z + 1), device_id_type=MESH)

    loads[0].wait()
    loads[1].wait()
    vals = jnp.sqrt(lib_ref[0].astype(jnp.float32))
    total = jnp.sum(vals * vals, axis=-1, keepdims=True)
    mine = pl.ds(pl.multiple_of(b * rows, rows), rows)
    lib[z, mine, 0:W] = (vals * lax.rsqrt(total + 1e-06)).astype(jnp.bfloat16)
    r_id = lax.broadcasted_iota(jnp.int32, (rows, rows), 0)
    c_id = lax.broadcasted_iota(jnp.int32, (rows, rows), 1)
    spread = jnp.where(r_id == c_id, libbin_ref[...].astype(jnp.float32), 0.0)
    own_bins = jnp.sum(spread, axis=1, keepdims=True)
    lib[z, mine, W : W + LANES] = jnp.broadcast_to(own_bins, (rows, LANES)).astype(jnp.bfloat16)

    ends = jnp.where(z == 0, 1, 0) + jnp.where(z == n_rep - 1, 1, 0)
    pl.semaphore_wait(barrier, 5 - ends)

    def order(j):
        m = z // (n_rep // 2)
        zz = z + m * (n_rep - 1 - 2 * z)
        o = jnp.where(j == 0, zz, jnp.where(j == 1, 1 - zz, j))
        return o + m * (n_rep - 1 - 2 * o)

    def shard(p, blk):
        return lib.at[p, pl.ds(pl.multiple_of(blk * rows, rows), rows)]

    split = (W // 2 + LANES, W // 2)

    def part(p, blk, h, c):
        at = pl.ds(pl.multiple_of(blk * rows + h * half, half), half)
        return lib.at[p, at, pl.ds(c * split[0], split[c])]

    def copy(ref, send, recv, dev):
        return pltpu.make_async_remote_copy(
            src_ref=ref, dst_ref=ref, send_sem=send, recv_sem=recv,
            device_id=dev, device_id_type=MESH,
        )

    def z_up(p):
        return copy(shard(p, b), zs.at[0, p], zr.at[p], (b, z + 1))

    def z_down(p):
        return copy(shard(p, b), zs.at[1, p], zr.at[p], (b, z - 1))

    def x_own(p, blk):
        return copy(shard(p, blk), xs.at[p], xr.at[p], (xn, z))

    def y_own(p, blk):
        return copy(shard(p, blk), ys.at[p], yr.at[p], (yn, z))

    def x_diag(p, blk):
        return copy(part(p, blk, 1, 1), xds.at[p], xdr.at[p], (xn, z))

    def y_diag(p, blk):
        return copy(part(p, blk, 1, 0), yds.at[p], ydr.at[p], (yn, z))

    def x_home(blk):
        return copy(part(z, blk, 0, 1), hs.at[0], hr.at[0], (xn, z))

    def y_home(blk):
        return copy(part(z, blk, 0, 0), hs.at[1], hr.at[1], (yn, z))

    def top_half(p):
        return lib.at[p, pl.ds(pl.multiple_of(dn * rows, half), half)]

    def zd_up(p):
        return copy(top_half(p), zds.at[0, p], zdr.at[p], (b, z + 1))

    def zd_down(p):
        return copy(top_half(p), zds.at[1, p], zdr.at[p], (b, z - 1))

    def to_sib(p, blk, slot):
        return copy(shard(p, blk), ss.at[p, slot], sr.at[p, slot], (sib, z))

    def away(p, up, down, do):
        @pl.when((p <= z) & (z < n_rep - 1))
        def _():
            do(up(p))

        @pl.when((p >= z) & (z > 0))
        def _():
            do(down(p))

    def begin(c):
        c.start()

    def spread_own(p):
        away(p, z_up, z_down, begin)
        x_own(p, b).start()
        y_own(p, b).start()
        to_sib(p, b, 0).start()

    def column(t):
        p = order(t)
        z_up(p).wait_recv()
        spread_own(p)

    spread_own(z)

    for c in loads[2:]:
        c.wait()
    step = 512

    def load(i, acc):
        cols = pl.ds(pl.multiple_of(i * step, step), step)
        v = jnp.sqrt(qraw[:, cols].astype(jnp.float32).T)
        qval[cols, :] = v
        return acc + jnp.sum(v * v, axis=0, keepdims=True)

    n_q = qraw.shape[0]
    q_total = lax.fori_loop(0, W // step, load, jnp.zeros((1, n_q), jnp.float32))
    scale = lax.rsqrt(q_total + 1e-06)

    x_own(z, b).wait_recv()
    y_home(xn).start()
    y_own(z, b).wait_recv()
    x_home(yn).start()
    y_diag(z, xn).start()
    to_sib(z, xn, 1).start()
    x_diag(z, yn).start()
    to_sib(z, yn, 2).start()
    column(1)

    def norm(i, c):
        at = pl.ds(pl.multiple_of(i * step, step), step)
        qt[at, 0:n_q] = (qval[at, :] * scale).astype(jnp.bfloat16)
        return c

    lax.fori_loop(0, W // step, norm, 0)
    qt[pl.ds(W, 2 * SHIFT_BINS), 0:n_q] = jnp.zeros((2 * SHIFT_BINS, n_q), jnp.bfloat16)
    one = shift_ref[...] == 1

    def move(i, c):
        base = pl.multiple_of(i * step, step)
        near = qt[pl.ds(base + SHIFT_BINS, step), 0:n_q].astype(jnp.float32)
        far = qt[pl.ds(base + 2 * SHIFT_BINS, step), 0:n_q].astype(jnp.float32)
        qt[pl.ds(base, step), n_q : 2 * n_q] = jnp.where(one, near, far).astype(jnp.bfloat16)
        return c

    lax.fori_loop(0, W // step, move, 0)
    best[...] = jnp.zeros_like(best)

    def compute(p):
        for slot, blk in enumerate((b, xn, yn, dn)):
            to_sib(p, blk, slot).wait_recv()
        prod = jnp.dot(lib[p, :, 0:W], qt[0:W, :], preferred_element_type=jnp.float32)
        high = jnp.maximum(prod[:, 0:n_q], prod[:, n_q : 2 * n_q])
        bins = lib[p, :, W : W + LANES].astype(jnp.float32)
        bins = jnp.concatenate([bins] * (n_q // LANES), axis=1)
        near = jnp.abs(bins - bin_ref[...].astype(jnp.float32)) <= float(WIN)
        score = jnp.where(near, high, 0.0)
        best[...] = jnp.where(grp_ref[...] == p, score, best[...])

    def stage(t, c):
        @pl.when(t < n_rep)
        def _():
            column(t)

        @pl.when(t <= n_rep)
        def _():
            p = order(t - 1)
            x_own(p, b).wait_recv()
            y_diag(p, xn).start()
            to_sib(p, xn, 1).start()
            y_own(p, b).wait_recv()
            x_diag(p, yn).start()
            to_sib(p, yn, 2).start()

        @pl.when(t == 2)
        def _():
            x_home(dn).wait_recv()
            y_home(dn).wait_recv()
            away(z, zd_up, zd_down, begin)

        @pl.when(t <= n_rep)
        def _():
            p = order(t - 1)
            zd_up(p).wait_recv()
            away(p, zd_up, zd_down, begin)

        @pl.when(t <= n_rep + 1)
        def _():
            p = order(t - 2)
            x_diag(p, dn).wait_recv()
            y_diag(p, dn).wait_recv()
            to_sib(p, dn, 3).start()

        @pl.when(t >= 3)
        def _():
            compute(order(t - 3))

        return c

    lax.fori_loop(2, n_rep + 3, stage, 0)

    position = lax.broadcasted_iota(jnp.int32, (K, n_q), 0)
    result = jnp.zeros((K, n_q), jnp.float32)
    filled = jnp.zeros((1, n_q), jnp.int32)
    for _ in range(K):
        cur = best[...]
        top = jnp.max(cur, axis=0, keepdims=True)
        same = cur == top
        count = jnp.sum(same.astype(jnp.int32), axis=0, keepdims=True)
        best[...] = jnp.where(same, -3e38, cur)
        result = jnp.where(position >= filled, top, result)
        filled = filled + count
    out_ref[...] = result

    def finish(p, c):
        away(p, z_up, z_down, lambda d: d.wait_send())
        away(p, zd_up, zd_down, lambda d: d.wait_send())
        x_own(p, b).wait_send()
        y_own(p, b).wait_send()
        y_diag(p, xn).wait_send()
        x_diag(p, yn).wait_send()
        for slot, blk in enumerate((b, xn, yn, dn)):
            to_sib(p, blk, slot).wait_send()
        return c

    lax.fori_loop(0, n_rep, finish, 0)
    x_home(yn).wait_send()
    y_home(xn).wait_send()


def fast(n_rep, queries, query_group, query_bin, query_shift, library, library_bin):
    n_q = queries.shape[0]
    rows = library.shape[1]
    lib_g = 8 * rows
    dma = pltpu.SemaphoreType.DMA
    vmem = pl.BlockSpec(memory_space=pltpu.VMEM)
    top = pl.pallas_call(
        functools.partial(fast_kernel, n_rep, rows),
        out_shape=jax.ShapeDtypeStruct((K, n_q), jnp.float32),
        in_specs=[pl.BlockSpec(memory_space=pltpu.HBM)] * 6,
        out_specs=vmem,
        scratch_shapes=[
            pltpu.VMEM((n_rep, lib_g, W + LANES), jnp.bfloat16),
            pltpu.VMEM((n_q, W), jnp.bfloat16),
            pltpu.VMEM((W, n_q), jnp.float32),
            pltpu.VMEM((W + 2 * SHIFT_BINS, 2 * n_q), jnp.bfloat16),
            pltpu.VMEM((lib_g, n_q), jnp.float32),
            pltpu.VMEM((1, rows, W), jnp.bfloat16),
            pltpu.VMEM((1, rows), jnp.int32),
            pltpu.VMEM((1, n_q), jnp.int32),
            pltpu.VMEM((1, n_q), jnp.int32),
            pltpu.VMEM((1, n_q), jnp.int32),
            dma((6,)),
            dma((2, n_rep)), dma((n_rep,)),
            dma((n_rep,)), dma((n_rep,)), dma((n_rep,)), dma((n_rep,)),
            dma((n_rep,)), dma((n_rep,)), dma((n_rep,)), dma((n_rep,)),
            dma((n_rep, 4)), dma((n_rep, 4)),
            dma((2, n_rep)), dma((n_rep,)), dma((2,)), dma((2,)),
        ],
        compiler_params=pltpu.CompilerParams(
            collective_id=0, has_side_effects=True, vmem_limit_bytes=64 * 1024 * 1024 - 65536
        ),
    )(
        queries,
        library,
        library_bin,
        query_group.reshape(1, n_q),
        query_bin.reshape(1, n_q),
        query_shift.reshape(1, n_q),
    )
    return top.T


def solution(mesh):
    in_specs = (
        P(("blk", "rep"), None),
        P(("blk", "rep"), None),
        P(("blk", "rep")),
        P(("blk", "rep")),
        P("rep", "blk", None),
        P("rep", "blk"),
    )
    out_specs = P(("blk", "rep"), None)
    if mesh.shape["blk"] == 8 and mesh.shape["rep"] == 4:
        body = functools.partial(fast, mesh.shape["rep"])
    else:
        body = general
    return jax.shard_map(
        body, mesh=mesh, in_specs=in_specs, out_specs=out_specs, check_vma=False
    )
```
